128 devices in a mesh: dp: 64 (over z, y, x), inner: 2 (over core).
Axes of the slice: x: 4, y: 4, z: 4, core: 2. Of those that a mesh axis runs over, the one named last changes fastest.
Arguments:
- latent_pool: bfloat16 [8192, 64, 576], P('dp', 'inner'), may hold values from -7 to 7
- block_table: int32 [2, 512, 8], P(None, 'dp'), may hold values from 0 to 127, as said below
- cache_lengths: int32 [2, 512], P(None, 'dp'), may hold values from 2 to 512
- queries: bfloat16 [2, 512, 128, 576], P(None, 'dp', 'inner'), may hold values from -400 to 400
- hidden_states: bfloat16 [2, 512, 3584], P(None, 'dp', 'inner'), may hold values from -6 to 6
- expert_ids: int32 [2, 512, 8], P(None, 'dp'), may hold values from 0 to 63, all different within a row; in each aligned block of 8 rows (0 to 7, 8 to 15, ..., all dimensions but the last counted through in order) at most 2 rows name the same one
- gate_weights: float32 [2, 512, 8], P(None, 'dp'), may hold values from 0.05 to 0.6
- w_gate: bfloat16 [64, 3584, 1024], P('dp', None, 'inner'), may hold values from -0.09375 to 0.09375
- w_up: bfloat16 [64, 3584, 1024], P('dp', None, 'inner'), may hold values from -0.09375 to 0.09375
- w_down: bfloat16 [64, 1024, 3584], P('dp', 'inner'), may hold values from -0.1875 to 0.1875
Outputs:
- context: bfloat16 [2, 512, 128, 512], P(None, 'dp', 'inner')
- moe_out: bfloat16 [2, 512, 3584], P(None, 'dp', 'inner')
The draws below stay inside these ranges and needn't reach their ends.
Inputs may be any that keep to these rules, and one draw needn't show every extreme that they name: `block_table`: over both micro-batches, the 128 entries of the sessions of one dp index name every slot exactly once; entries of blocks past a session's length are never read. `expert_ids`: in each micro-batch, at most 2 of the tokens of one dp index name the same expert, and no token names one expert twice.
All inputs are finite; a program needn't handle non-finite values.
Results may differ from the reference program's by a relative error of at most 0.018.
Values may be sent and summed in bfloat16 or wider, within the bound.
A program may use at most 128 MiB of HBM per device.

```python
import math
import jax
import jax.numpy as jnp
import numpy as np
from jax import lax

D = 3584
FFE = 1024
H = 128
KV = 512
TOPK = 8
BLK = 64
MAXB = 8
MB = 2
SESS_DEV = 8
SESSIONS = 512
EXPERTS = 64
CAP = 2
CAPB = 2
C = 576
N_DP = 64
N_INNER = 2


def permute_one(subkey):
    return jax.random.permutation(subkey, MB * SESS_DEV * MAXB)


def shared_table(key):
    subkeys = jax.random.split(jax.random.fold_in(key, 11), N_DP)
    permuted = jax.vmap(permute_one)(subkeys)
    slot_table = permuted.reshape(N_DP, MB, SESS_DEV, MAXB).transpose(1, 0, 2, 3)
    return slot_table.reshape(MB, SESSIONS, MAXB).astype(jnp.int32)


def shared_latent(key):
    latent_base = jax.random.normal(jax.random.fold_in(key, 13), (N_DP * N_DP * CAPB, BLK, C), jnp.float32)
    return jnp.clip(latent_base, -6.0, 6.0)


def draw_block_table(key, part):
    return shared_table(key)


def draw_latent_pool(key, part):
    latent_base = shared_latent(key)
    return latent_base.astype(jnp.bfloat16)


def draw_queries(key, part):
    key = jax.random.fold_in(key, 5)
    drawn = jnp.clip(jax.random.normal(key, (MB, SESSIONS, H, C), jnp.float32), -6.0, 6.0)
    return drawn.astype(jnp.bfloat16)


def draw_cache_lengths(key, part):
    key = jax.random.fold_in(key, 2)
    longest_len = MAXB * BLK
    level = jax.random.randint(jax.random.fold_in(key, 1), (1, N_DP, 1), 2, longest_len + 1)
    uniform_draw = jax.random.randint(jax.random.fold_in(key, 2), (MB, N_DP, SESS_DEV), 0, longest_len)
    lengths = 2 + uniform_draw * (level - 1) // longest_len
    longest = jax.random.randint(jax.random.fold_in(key, 3), (), 0, MB * SESSIONS)
    lengths = lengths.reshape(MB * SESSIONS).at[longest].set(longest_len)
    return lengths.reshape(MB, SESSIONS).astype(jnp.int32)


def level_of(rng, extent, cuts, smallest, top_value):
    level = 1.0
    for axis_at, parts in cuts:
        draws = jax.random.uniform(jax.random.fold_in(jax.random.fold_in(rng, 6), axis_at), (parts,), jnp.float32, smallest / len(cuts), top_value / len(cuts))
        level = level * jnp.repeat(jnp.exp(draws), extent[axis_at] // parts).reshape((-1,) + (1,) * (len(extent) - 1 - axis_at))
    return level


def shared_out(own_key, own, number, rows, count, top, limit, skew):
    sequence = jax.random.permutation(own_key, count)
    crowded, usual = load_shares(count, rows * top, limit, skew, True), load_shares(count, rows * top, limit, skew, False)
    places = jnp.arange(count)

    def named(tallies, rotation):
        used = int((tallies > 0).sum())
        fixed = max(1, used // 4)
        shifted = fixed + (places - fixed + rotation * (used - fixed)) % max(1, count - fixed)
        return jnp.zeros((count,), jnp.int32).at[sequence[jnp.where(places < fixed, places, shifted)]].set(jnp.asarray(tallies, jnp.int32))

    tallies = jnp.where(number % 4 == 0, named(crowded, number // 4), named(usual, number - number // 4 - 1))
    mixed = jax.random.permutation(jax.random.fold_in(own, 3), count)
    donor, taker = mixed[0:count // 2 * 2:2], mixed[1:count // 2 * 2:2]
    slack = jnp.minimum(tallies[donor] - 1, limit - tallies[taker]) // 2
    slack = jnp.where((donor == sequence[0]) | (taker == sequence[0]) | (tallies[taker] == 0), 0, jnp.maximum(slack, 0))
    shifted = jax.random.randint(jax.random.fold_in(own, 4), (count // 2,), 0, 1 << 20) % (slack + 1)
    tallies = tallies.at[donor].add(-shifted).at[taker].add(shifted)
    items = jnp.searchsorted(jnp.cumsum(tallies), jnp.arange(rows * top), side="right").astype(jnp.int32)
    table = items.reshape(top, rows).T
    table = table[jax.random.permutation(jax.random.fold_in(own, 1), rows)]
    rotation = jax.random.randint(jax.random.fold_in(own, 2), (rows, 1), 0, top)
    return jnp.take_along_axis(table, (jnp.arange(top)[None, :] + rotation) % top, axis=1)


def load_shares(number_of, total, most, lean, full):
    weights = [(1 << 20) // math.isqrt(grade ** lean) + 1 for grade in range(1, number_of + 1)]
    largest = most if full else min(most, max(-(-total // number_of), total * weights[0] // sum(weights)))
    least = 1 if total - largest >= number_of - 1 else 0
    given, surplus = [largest] + [least] * (number_of - 1), total - largest - least * (number_of - 1)
    while surplus > 0:
        candidates = [i for i in range(1, number_of) if given[i] < largest] or [i for i in range(1, number_of) if given[i] < most]
        whole, budget = sum([weights[i] for i in candidates]), surplus
        for i in candidates:
            extra = min(most - given[i], max(1, budget * weights[i] // whole), surplus)
            given[i] = given[i] + extra
            surplus = surplus - extra
    return np.array(given)


def centred(own_key, dims, deviation, limit, cuts=(), kind=jnp.bfloat16):
    array = deviation * jax.random.normal(own_key, dims, jnp.float32)
    if cuts:
        array = array * level_of(own_key, dims, cuts, -0.22, 0.18)
    return jnp.clip(array, -limit, limit).astype(kind)


def setup_inputs(seed: int = 0) -> dict:
    streams_of = jax.random.split(jax.random.key(seed), 11)
    latent_pool = draw_latent_pool(jax.random.fold_in(streams_of[10], 71), 0)
    block_table = draw_block_table(jax.random.fold_in(streams_of[10], 71), 0)
    cache_lengths = draw_cache_lengths(jax.random.fold_in(streams_of[10], 71), 0)
    queries = draw_queries(jax.random.fold_in(streams_of[10], 71), 0)
    hidden_states = centred(streams_of[4], (MB, SESSIONS, D), 1.0, 6.0, ((1, 64), (2, 2)))
    expert_ids_keys = jax.random.split(jax.random.fold_in(streams_of[5], 1), MB * SESSIONS // SESS_DEV)
    expert_ids_turns = jax.random.permutation(jax.random.fold_in(streams_of[5], 3), MB * SESSIONS // SESS_DEV)
    expert_ids = jax.vmap(lambda own, number: shared_out(jax.random.fold_in(streams_of[5], 2), own, number, SESS_DEV, EXPERTS, TOPK, CAP, 2))(expert_ids_keys, expert_ids_turns).reshape((MB, SESSIONS, TOPK))
    gate_weights = jnp.clip(jnp.exp(math.log(0.6) - 2.4849067 * jax.random.uniform(streams_of[6], (MB, SESSIONS, TOPK), jnp.float32) ** level_of(streams_of[6], (MB, SESSIONS, TOPK), ((1, 64),), -0.2, 0.2)), 0.05, 0.6)
    w_gate = centred(streams_of[7], (EXPERTS, D, FFE), D ** -0.5, 0.09375, ((0, 64), (2, 2)))
    w_up = centred(streams_of[8], (EXPERTS, D, FFE), D ** -0.5, 0.09375, ((0, 64), (2, 2)))
    w_down = centred(streams_of[9], (EXPERTS, FFE, D), FFE ** -0.5, 0.1875, ((0, 64), (1, 2)))
    return dict(latent_pool=latent_pool, block_table=block_table, cache_lengths=cache_lengths, queries=queries, hidden_states=hidden_states, expert_ids=expert_ids, gate_weights=gate_weights, w_gate=w_gate, w_up=w_up, w_down=w_down)


softmax_scale = 192 ** -0.5


def reference(latent_pool, block_table, cache_lengths, queries, hidden_states, expert_ids, gate_weights, w_gate, w_up, w_down):
    session_count = MB * SESSIONS
    slot_table = block_table.reshape(session_count, MAXB)
    owner = (jnp.arange(session_count, dtype=jnp.int32) % SESSIONS) // SESS_DEV
    pool_rows = (slot_table // CAPB) * (N_DP * CAPB) + owner[:, None] * CAPB + slot_table % CAPB
    lengths = cache_lengths.reshape(session_count)
    flat_queries = queries.reshape(session_count, H, C)
    positions = jnp.arange(MAXB * BLK, dtype=jnp.int32)

    def attend(items):
        pool_index, length, query = items
        cache = latent_pool[pool_index].reshape(MAXB * BLK, C).astype(jnp.float32)
        scores = jnp.dot(query.astype(jnp.float32), cache.T, precision=lax.Precision.HIGHEST) * softmax_scale
        inside = positions < length
        scores = jnp.where(inside[None, :], scores, -jnp.inf)
        highest = jnp.max(scores, axis=1, keepdims=True)
        weights = jnp.where(inside[None, :], jnp.exp(scores - highest), 0.0)
        mass = jnp.sum(weights, axis=1, keepdims=True)
        mixed = jnp.dot(weights, cache[:, :KV], precision=lax.Precision.HIGHEST)
        return (mixed / mass).astype(jnp.bfloat16)

    context = lax.map(attend, (pool_rows, lengths, flat_queries)).reshape(MB, SESSIONS, H, KV)

    pair_count = MB * SESSIONS * TOPK
    chosen = expert_ids.reshape(pair_count)
    ordering = jnp.argsort(chosen, stable=True).astype(jnp.int32)
    sorted_ids = chosen[ordering]
    counts = jnp.zeros((EXPERTS,), jnp.int32).at[chosen].add(1)
    starts = (jnp.cumsum(counts) - counts).astype(jnp.int32)
    capacity = MB * N_DP * CAP
    tokens = hidden_states.reshape(MB * SESSIONS, D)
    lined = tokens[ordering // TOPK]
    lined = jnp.concatenate([lined, jnp.zeros((capacity, D), jnp.bfloat16)], axis=0)
    group_width = FFE // N_INNER

    def expert(expert_id):
        block_rows = lax.dynamic_slice_in_dim(lined, starts[expert_id], capacity, 0)
        gate = jnp.dot(block_rows, w_gate[expert_id], preferred_element_type=jnp.float32)
        up = jnp.dot(block_rows, w_up[expert_id], preferred_element_type=jnp.float32)
        hidden = (jax.nn.silu(gate) * up).astype(jnp.bfloat16)
        pieces = jnp.einsum("rgf,gfd->rgd", hidden.reshape(capacity, N_INNER, group_width).astype(jnp.float32),
                            w_down[expert_id].reshape(N_INNER, group_width, D).astype(jnp.float32),
                            precision=lax.Precision.HIGHEST)
        partial_value = lax.optimization_barrier(pieces.astype(jnp.bfloat16)).astype(jnp.float32)
        return jnp.sum(partial_value, axis=1).astype(jnp.bfloat16)

    outputs = lax.map(expert, jnp.arange(EXPERTS, dtype=jnp.int32))
    slot_index = jnp.arange(pair_count, dtype=jnp.int32) - starts[sorted_ids]
    picked = outputs[sorted_ids, slot_index]
    placed = jnp.zeros((pair_count, D), jnp.bfloat16).at[ordering].set(picked)
    weighted = placed.reshape(MB * SESSIONS, TOPK, D).astype(jnp.float32) * gate_weights.reshape(MB * SESSIONS, TOPK, 1)
    moe_out = jnp.sum(weighted, axis=1).astype(jnp.bfloat16).reshape(MB, SESSIONS, D)
    return context, moe_out
```

```python
import functools

import jax
import jax.numpy as jnp
from jax import lax
from jax.experimental import pallas as pl
from jax.experimental.pallas import tpu as pltpu
from jax.sharding import PartitionSpec as P

MESH = pl.DeviceIdType.MESH
BF16, F32 = jnp.bfloat16, jnp.float32
SCALE = 192 ** (-0.5)
N = 64
POS = 32
KV, TAIL = 512, 64
SLOT = 144
SESS = 16
HEADS = 64
ROW = 16
CHUNK = 512
SLICE = 1792
NEG = -1e30
WIDTHS = (512, 512, 512, 256)
DIST = (0, 1, 2, 1)


def dot(a, b):
    return jnp.dot(a, b, preferred_element_type=F32)


def dot_t(a, b):
    return lax.dot_general(a, b, (((1,), (1,)), ((), ())), preferred_element_type=F32)


def target_orders():
    every = [(i % 4, i // 4 % 4, i // 16) for i in range(1, N)]
    kind = lambda o: tuple(sorted((DIST[a] for a in o), reverse=True))
    flip = lambda o: tuple(-a % 4 for a in o)
    turn = lambda o: (o[1], o[2], o[0])
    order = []
    for k in sorted({kind(o) for o in every}, key=lambda k: (-sum(k), k)):
        seen = []
        for o in every:
            if kind(o) != k or o in seen:
                continue
            for _ in range(3):
                for q in (o, flip(o)):
                    if q not in seen:
                        seen.append(q)
                o = turn(o)
        order += seen
    return order, [turn(o) for o in order]


ORDERS = target_orders()


def iota(shape, dim):
    return lax.broadcasted_iota(jnp.int32, shape, dim)


def kernel(
    table, lengths, pool, queries, tokens, ids, gates, w_gate, w_up, w_down,
    context, moe,
    raw, wide, packed, resident, q_all, wg, wu, wd, out_rows, in_rows, in_other,
    share_out, share_in, back_rows, ret_rows, part_own, lse_own, part_out, lse_out, part_in, lse_in,
    raw_sem, w_sem, q_sem, pool_send, pool_recv, disp_send, disp_recv, back_send, back_recv,
    pair_send, pair_recv, part_send, part_recv, lse_send, lse_recv,
):
    me = lax.axis_index("dp")
    core = lax.axis_index("inner")
    z, y, x = me // 16, me // 4 % 4, me % 4

    def shifted(o, sign):
        return (z + sign * o[2]) % 4 * 16 + (y + sign * o[1]) % 4 * 4 + (x + sign * o[0]) % 4

    def peer(i, sign):
        a, b = shifted(ORDERS[0][i], sign), shifted(ORDERS[1][i], sign)
        return a + core * (b - a)

    sibling = {"inner": 1 - core}

    loads = []
    for k in range(4):
        for half in range(2):
            rows = pl.ds(half * 16 + k * 4, 4)
            loads.append(pltpu.make_async_copy(pool.at[rows], raw.at[rows], raw_sem.at[k * 2 + half]))
    for c in loads:
        c.start()
    q_own = pltpu.make_async_copy(queries, q_all.at[0], q_sem.at[0])
    q_own.start()
    weights = [
        pltpu.make_async_copy(a, b, w_sem.at[i]) for i, (a, b) in enumerate(((w_gate, wg), (w_up, wu), (w_down, wd)))
    ]
    for c in weights:
        c.start()

    barrier = pltpu.get_barrier_semaphore()

    def greet(i, carry):
        pl.semaphore_signal(barrier, inc=1, device_id={"dp": (me + i) % N}, device_id_type=MESH)
        return carry

    lax.fori_loop(1, N, greet, 0)
    pl.semaphore_signal(barrier, inc=1, device_id=sibling, device_id_type=MESH)

    experts = iota((SESS, N), 1)
    member, weight = jnp.zeros((SESS, N), F32), jnp.zeros((SESS, N), F32)
    for k in range(8):
        same = ids[:, k : k + 1] == experts
        member += jnp.where(same, 1.0, 0.0)
        weight += jnp.where(same, gates[:, k : k + 1], 0.0)
    r, c = iota((SESS, SESS), 0), iota((SESS, SESS), 1)
    before = dot(jnp.where((c < r) & (c // 8 == r // 8), 1.0, 0.0).astype(BF16), member.astype(BF16))
    tokens4 = jnp.concatenate(
        [tokens[:, 0:512], tokens[:, 512:1024], tokens[:, 1024:1536],
         jnp.concatenate([tokens[:, 1536:1792], jnp.zeros((SESS, 256), BF16)], axis=1)], axis=0)
    picks = [jnp.where(before == j, member, 0.0) for j in range(2)]
    name = jnp.where(iota((N * ROW, N), 0) // ROW == iota((N * ROW, N), 1), 1.0, 0.0).astype(BF16)

    def spread(m):
        return jnp.concatenate([m] * 4, axis=0).astype(BF16)

    rr, cc = iota((N * ROW, N), 0), iota((N * ROW, N), 1)
    fits = (rr % ROW // 4 == cc // SESS) & (rr % 2 == cc % SESS // 8)
    chosen = jnp.where(rr % 4 // 2 == 0, dot_t(name, spread(picks[0])), dot_t(name, spread(picks[1])))
    placing = jnp.where(fits, chosen, 0.0).astype(BF16)
    out_rows[...] = dot(placing, tokens4).astype(BF16)

    eye = jnp.where(iota((128, 128), 0) == iota((128, 128), 1), 1.0, 0.0).astype(BF16)
    for k in range(4):
        loads[2 * k].wait()
        loads[2 * k + 1].wait()

        def turn(n, carry, k=k):
            j = k * 4 + n
            for jj in (j, j + 16):
                flat = dot_t(eye, raw[jj, 0:KV, :])
                for i in range(4):
                    wide[pl.ds(i * POS + jj, 128, SLOT), :] = flat[:, i * 128 : (i + 1) * 128]
            rest = jnp.concatenate([raw[j, KV:, :], raw[j + 16, KV:, :]], axis=0)
            wide[pl.ds(4 * POS + j, 128, SLOT), :] = dot_t(eye, rest)
            return carry

        lax.fori_loop(0, 4, turn, 0)

    pl.semaphore_wait(barrier, N)

    def dispatch(i):
        d = peer(i, 1)
        return pltpu.make_async_remote_copy(
            src_ref=out_rows.at[pl.ds(pl.multiple_of(d * ROW, ROW), ROW)],
            dst_ref=in_rows.at[pl.ds(pl.multiple_of(me * ROW, ROW), ROW)],
            send_sem=disp_send.at[i], recv_sem=disp_recv.at[i], device_id={"dp": d}, device_id_type=MESH)

    for i in range(N - 1):
        dispatch(i).start()
    q_own.wait()
    q_copy = pltpu.make_async_remote_copy(
        src_ref=q_all.at[0], dst_ref=q_all.at[1], send_sem=pair_send.at[0], recv_sem=pair_recv.at[0],
        device_id=sibling, device_id_type=MESH)
    q_copy.start()

    def exchange(i):
        d = peer(i, 1)
        return pltpu.make_async_remote_copy(
            src_ref=packed.at[d], dst_ref=resident.at[pl.ds(me * 2, 2)],
            send_sem=pool_send.at[i], recv_sem=pool_recv.at[i], device_id={"dp": d}, device_id_type=MESH)

    for i in range(N - 1):
        d = peer(i, 1)
        for h in range(2):
            packed[d, h] = wide[pl.ds(pl.multiple_of((d * 2 + h) * SLOT, SLOT), SLOT), :].astype(BF16)
        exchange(i).start()
    for h in range(2):
        resident[me * 2 + h] = wide[pl.ds(pl.multiple_of((me * 2 + h) * SLOT, SLOT), SLOT), :].astype(BF16)
    own = pl.ds(pl.multiple_of(me * ROW, ROW), ROW)
    in_rows[own, :] = out_rows[own, :]

    for i in range(N - 1):
        dispatch(i).wait()
    pair = pltpu.make_async_remote_copy(
        src_ref=in_rows, dst_ref=in_other, send_sem=pair_send.at[1], recv_sem=pair_recv.at[1],
        device_id=sibling, device_id_type=MESH)
    pair.start()
    r, c = iota((256, 256), 0), iota((256, 256), 1)
    order = r // 64 * 4 + r % 64 // 4 * 16 + r % 4
    gather = jnp.where(c == order, 1.0, 0.0).astype(BF16)
    scatter = jnp.where(r == c // 64 * 4 + c % 64 // 4 * 16 + c % 4, 1.0, 0.0).astype(BF16)
    for c_ in weights:
        c_.wait()
    gate_sum, up_sum = jnp.zeros((256, 512), F32), jnp.zeros((256, 512), F32)
    for side in range(2):
        if side == 1:
            pair.wait()
        rows_ref = (in_rows, in_other)[side]
        half = core if side == 0 else 1 - core
        lined = [dot(gather, rows_ref[k * 256 : (k + 1) * 256, :]).astype(BF16) for k in range(4)]
        for q, width in enumerate(WIDTHS):
            part = jnp.concatenate([lined[k][q * 64 : (q + 1) * 64, :width] for k in range(4)], axis=0)
            rows = pl.ds(pl.multiple_of(half * SLICE + q * CHUNK, 256), width)
            gate_sum += dot(part, wg[rows, :])
            up_sum += dot(part, wu[rows, :])
    hidden = (gate_sum / (1.0 + jnp.exp(-gate_sum)) * up_sum).astype(BF16)
    for q, width in enumerate(WIDTHS):
        columns = pl.ds(pl.multiple_of((1 - core) * SLICE + q * CHUNK, 256), width)
        share_out[:, q * CHUNK : q * CHUNK + width] = dot(hidden, wd[:, columns]).astype(BF16)
    share = pltpu.make_async_remote_copy(
        src_ref=share_out, dst_ref=share_in, send_sem=pair_send.at[2], recv_sem=pair_recv.at[2],
        device_id=sibling, device_id_type=MESH)
    share.start()
    mine = []
    for q, width in enumerate(WIDTHS):
        columns = pl.ds(pl.multiple_of(core * SLICE + q * CHUNK, 256), width)
        mine.append(dot(hidden, wd[:, columns]).astype(BF16))
    share.wait()
    full = []
    for q, width in enumerate(WIDTHS):
        total = (mine[q].astype(F32) + share_in[:, q * CHUNK : q * CHUNK + width].astype(F32)).astype(BF16)
        if width < CHUNK:
            total = jnp.concatenate([total, jnp.zeros((256, CHUNK - width), BF16)], axis=1)
        full.append(total)
    for k in range(4):
        stacked = jnp.concatenate([full[q][k * 64 : (k + 1) * 64] for q in range(4)], axis=0)
        back_rows[k * 256 : (k + 1) * 256, :] = dot(scatter, stacked).astype(BF16)

    def send_back(i):
        d = peer(i, 1)
        return pltpu.make_async_remote_copy(
            src_ref=back_rows.at[pl.ds(pl.multiple_of(d * ROW, ROW), ROW)],
            dst_ref=ret_rows.at[pl.ds(pl.multiple_of(me * ROW, ROW), ROW)],
            send_sem=back_send.at[i], recv_sem=back_recv.at[i], device_id={"dp": d}, device_id_type=MESH)

    for i in range(N - 1):
        send_back(i).start()
    ret_rows[own, :] = back_rows[own, :]

    q_copy.wait()
    for i in range(N - 1):
        exchange(i).wait()

    col = iota((2 * HEADS, 256), 1)
    position = col % 128 // 16 * 64 + core * POS + col // 128 * 16 + col % 16

    def parts(t):
        a = pltpu.make_async_remote_copy(
            src_ref=part_out.at[t], dst_ref=part_in.at[t], send_sem=part_send.at[t], recv_sem=part_recv.at[t],
            device_id=sibling, device_id_type=MESH)
        b = pltpu.make_async_remote_copy(
            src_ref=lse_out.at[t], dst_ref=lse_in.at[t], send_sem=lse_send.at[t], recv_sem=lse_recv.at[t],
            device_id=sibling, device_id_type=MESH)
        return a, b

    def attend(t, carry):
        low, high, rest = [], [], []
        for b in range(8):
            block = resident[table[t, b]]
            low.append(jnp.concatenate([block[i * POS : i * POS + 16] for i in range(4)], axis=1))
            high.append(jnp.concatenate([block[i * POS + 16 : i * POS + 32] for i in range(4)], axis=1))
            rest.append(block[4 * POS :])
        keys = jnp.concatenate(low + high, axis=0)
        rest = jnp.concatenate(rest, axis=0)
        q = jnp.concatenate([q_all[0, t], q_all[1, t]], axis=0)
        q_rest, blank = q[:, KV:], jnp.zeros((2 * HEADS, TAIL), BF16)
        scores = dot_t(q[:, :KV], keys) + jnp.concatenate(
            [dot_t(jnp.concatenate([q_rest, blank], axis=1), rest),
             dot_t(jnp.concatenate([blank, q_rest], axis=1), rest)], axis=1)
        inside = position < lengths[t]
        scores = jnp.where(inside, scores * SCALE, NEG)
        peak = jnp.max(scores, axis=1, keepdims=True)
        weights_ = jnp.where(inside, jnp.exp(scores - peak), 0.0)
        total = jnp.maximum(jnp.sum(weights_, axis=1, keepdims=True), 1e-30)
        value = dot(weights_.astype(BF16), keys) / total
        lse = jnp.broadcast_to(peak + jnp.log(total), (2 * HEADS, 128))
        part_own[t] = value[:HEADS]
        lse_own[t] = lse[:HEADS]
        part_out[t] = value[HEADS:].astype(BF16)
        lse_out[t] = lse[HEADS:]
        for copy in parts(t):
            copy.start()
        return carry

    lax.fori_loop(0, SESS, attend, 0)

    def merge(t, carry):
        for copy in parts(t):
            copy.wait()
        share_ = 1.0 / (1.0 + jnp.exp(lse_in[t] - lse_own[t]))
        share_ = jnp.concatenate([share_] * 4, axis=1)
        context[t] = (part_own[t] * share_ + part_in[t].astype(F32) * (1.0 - share_)).astype(BF16)
        return carry

    lax.fori_loop(0, SESS, merge, 0)

    for i in range(N - 1):
        send_back(i).wait()
    rr, cc = iota((N, N * ROW), 0), iota((N, N * ROW), 1)
    fits = (cc % ROW // 4 == rr // SESS) & (cc % 2 == rr % SESS // 8)
    shares = [jnp.where(before == j, weight, 0.0) for j in range(2)]
    total = jnp.zeros((N, CHUNK), F32)
    for level in range(2):
        tops = [s.astype(BF16) for s in shares]
        chosen = jnp.where(cc % 4 // 2 == 0, dot_t(spread(tops[0]), name), dot_t(spread(tops[1]), name))
        total += dot(jnp.where(fits, chosen, 0.0).astype(BF16), ret_rows[...])
        shares = [s - t_.astype(F32) for s, t_ in zip(shares, tops)]
    for q, width in enumerate(WIDTHS):
        moe[:, q * CHUNK : q * CHUNK + width] = total[q * SESS : (q + 1) * SESS, :width].astype(BF16)


def on_device(pool, table, lengths, queries, hidden, ids, gates, w_gate, w_up, w_down):
    vmem = pl.BlockSpec(memory_space=pltpu.VMEM)
    smem = pl.BlockSpec(memory_space=pltpu.SMEM)
    anywhere = pl.BlockSpec(memory_space=pl.ANY)
    dma = pltpu.SemaphoreType.DMA
    context, moe = pl.pallas_call(
        kernel,
        out_shape=(
            jax.ShapeDtypeStruct((SESS, HEADS, KV), BF16),
            jax.ShapeDtypeStruct((SESS, SLICE), BF16),
        ),
        in_specs=[smem, smem, anywhere, anywhere, vmem, vmem, vmem, anywhere, anywhere, anywhere],
        out_specs=(vmem, vmem),
        scratch_shapes=[
            pltpu.VMEM((POS, KV + TAIL, 128), BF16),
            pltpu.VMEM((128 * SLOT, 128), F32),
            pltpu.VMEM((N, 2, SLOT, 128), BF16),
            pltpu.VMEM((128, SLOT, 128), BF16),
            pltpu.VMEM((2, SESS, HEADS, KV + TAIL), BF16),
            pltpu.VMEM((2 * SLICE, 512), BF16),
            pltpu.VMEM((2 * SLICE, 512), BF16),
            pltpu.VMEM((512, 2 * SLICE), BF16),
            pltpu.VMEM((N * ROW, CHUNK), BF16),
            pltpu.VMEM((N * ROW, CHUNK), BF16),
            pltpu.VMEM((N * ROW, CHUNK), BF16),
            pltpu.VMEM((256, SLICE), BF16),
            pltpu.VMEM((256, SLICE), BF16),
            pltpu.VMEM((N * ROW, CHUNK), BF16),
            pltpu.VMEM((N * ROW, CHUNK), BF16),
            pltpu.VMEM((SESS, HEADS, KV), F32),
            pltpu.VMEM((SESS, HEADS, 128), F32),
            pltpu.VMEM((SESS, HEADS, KV), BF16),
            pltpu.VMEM((SESS, HEADS, 128), F32),
            pltpu.VMEM((SESS, HEADS, KV), BF16),
            pltpu.VMEM((SESS, HEADS, 128), F32),
            dma((8,)), dma((3,)), dma((1,)),
            dma((N,)), dma((N,)), dma((N,)), dma((N,)), dma((N,)), dma((N,)),
            dma((3,)), dma((3,)),
            dma((SESS,)), dma((SESS,)), dma((SESS,)), dma((SESS,)),
        ],
        compiler_params=pltpu.CompilerParams(
            collective_id=0, has_side_effects=True, vmem_limit_bytes=60 * 2**20
        ),
    )(
        table.reshape(SESS, 8), lengths.reshape(SESS), pool.transpose(1, 2, 0),
        queries.reshape(SESS, HEADS, KV + TAIL), hidden.reshape(SESS, SLICE),
        ids.reshape(SESS, 8), gates.reshape(SESS, 8), w_gate[0], w_up[0], w_down[0],
    )
    return context.reshape(2, 8, HEADS, KV), moe.reshape(2, 8, SLICE)


def solution(mesh):
    placed = (
        P("dp", "inner", None),
        P(None, "dp", None),
        P(None, "dp"),
        P(None, "dp", "inner", None),
        P(None, "dp", "inner"),
        P(None, "dp", None),
        P(None, "dp", None),
        P("dp", None, "inner"),
        P("dp", None, "inner"),
        P("dp", "inner", None),
    )
    return jax.shard_map(
        on_device,
        mesh=mesh,
        in_specs=placed,
        out_specs=(P(None, "dp", "inner", None), P(None, "dp", "inner")),
        check_vma=False,
    )
```

```python
import functools

import jax
import jax.numpy as jnp
from jax import lax
from jax.experimental import pallas as pl
from jax.experimental.pallas import tpu as pltpu
from jax.sharding import PartitionSpec as P

MESH = pl.DeviceIdType.MESH
BF16, F32 = jnp.bfloat16, jnp.float32
SCALE = 192 ** (-0.5)
N = 64
POS = 32
KV, TAIL = 512, 64
SLOT = 144
SESS = 16
HEADS = 64
ROW = 16
CHUNK = 512
SLICE = 1792
NEG = -1e30
WIDTHS = (512, 512, 512, 256)
DIST = (0, 1, 2, 1)


def dot(a, b):
    return jnp.dot(a, b, preferred_element_type=F32)


def dot_t(a, b):
    return lax.dot_general(a, b, (((1,), (1,)), ((), ())), preferred_element_type=F32)


def target_orders():
    every = [(i % 4, i // 4 % 4, i // 16) for i in range(1, N)]
    kind = lambda o: tuple(sorted((DIST[a] for a in o), reverse=True))
    flip = lambda o: tuple(-a % 4 for a in o)
    turn = lambda o: (o[1], o[2], o[0])
    order = []
    for k in sorted({kind(o) for o in every}, key=lambda k: (-sum(k), k)):
        seen = []
        for o in every:
            if kind(o) != k or o in seen:
                continue
            for _ in range(3):
                for q in (o, flip(o)):
                    if q not in seen:
                        seen.append(q)
                o = turn(o)
        order += seen
    return order, [turn(o) for o in order]


ORDERS = target_orders()


def iota(shape, dim):
    return lax.broadcasted_iota(jnp.int32, shape, dim)


def kernel(
    table, lengths, pool, queries, tokens, ids, gates, w_gate, w_up, w_down,
    context, moe,
    raw, wide, packed, resident, q_all, wg, wu, wd, out_rows, in_rows, in_other,
    share_out, share_in, back_rows, ret_rows, part_own, lse_own, part_out, lse_out, part_in, lse_in, shares_of,
    raw_sem, w_sem, q_sem, pool_send, pool_recv, disp_send, disp_recv, back_send, back_recv,
    pair_send, pair_recv, part_send, part_recv, lse_send, lse_recv,
):
    me = lax.axis_index("dp")
    core = lax.axis_index("inner")
    z, y, x = me // 16, me // 4 % 4, me % 4

    def shifted(o, sign):
        return (z + sign * o[2]) % 4 * 16 + (y + sign * o[1]) % 4 * 4 + (x + sign * o[0]) % 4

    def peer(i, sign):
        a, b = shifted(ORDERS[0][i], sign), shifted(ORDERS[1][i], sign)
        return a + core * (b - a)

    sibling = {"inner": 1 - core}

    barrier = pltpu.get_barrier_semaphore()

    def greet(i, carry):
        pl.semaphore_signal(barrier, inc=1, device_id={"dp": (me + i) % N}, device_id_type=MESH)
        return carry

    lax.fori_loop(1, N, greet, 0)
    pl.semaphore_signal(barrier, inc=1, device_id=sibling, device_id_type=MESH)

    loads = []
    for k in range(4):
        for half in range(2):
            rows = pl.ds(half * 16 + k * 4, 4)
            loads.append(pltpu.make_async_copy(pool.at[rows], raw.at[rows], raw_sem.at[k * 2 + half]))
    for c in loads:
        c.start()
    q_own = pltpu.make_async_copy(queries, q_all.at[0], q_sem.at[0])
    q_own.start()
    weights = [
        pltpu.make_async_copy(a, b, w_sem.at[i]) for i, (a, b) in enumerate(((w_gate, wg), (w_up, wu), (w_down, wd)))
    ]
    for c in weights:
        c.start()

    experts = iota((SESS, N), 1)
    member, weight = jnp.zeros((SESS, N), F32), jnp.zeros((SESS, N), F32)
    for k in range(8):
        same = ids[:, k : k + 1] == experts
        member += jnp.where(same, 1.0, 0.0)
        weight += jnp.where(same, gates[:, k : k + 1], 0.0)
    r, c = iota((SESS, SESS), 0), iota((SESS, SESS), 1)
    before = dot(jnp.where((c < r) & (c // 8 == r // 8), 1.0, 0.0).astype(BF16), member.astype(BF16))
    tokens4 = jnp.concatenate(
        [tokens[:, 0:512], tokens[:, 512:1024], tokens[:, 1024:1536],
         jnp.concatenate([tokens[:, 1536:1792], jnp.zeros((SESS, 256), BF16)], axis=1)], axis=0)
    picks = [jnp.where(before == j, member, 0.0) for j in range(2)]
    name = jnp.where(iota((N * ROW, N), 0) // ROW == iota((N * ROW, N), 1), 1.0, 0.0).astype(BF16)

    def spread(m):
        return jnp.concatenate([m] * 4, axis=0).astype(BF16)

    rr, cc = iota((N * ROW, N), 0), iota((N * ROW, N), 1)
    fits = (rr % ROW // 4 == cc // SESS) & (rr % 2 == cc % SESS // 8)
    chosen = jnp.where(rr % 4 // 2 == 0, dot_t(name, spread(picks[0])), dot_t(name, spread(picks[1])))
    placing = jnp.where(fits, chosen, 0.0).astype(BF16)
    out_rows[...] = dot(placing, tokens4).astype(BF16)

    pl.semaphore_wait(barrier, N)

    def dispatch(i):
        d = peer(i, 1)
        return pltpu.make_async_remote_copy(
            src_ref=out_rows.at[pl.ds(pl.multiple_of(d * ROW, ROW), ROW)],
            dst_ref=in_rows.at[pl.ds(pl.multiple_of(me * ROW, ROW), ROW)],
            send_sem=disp_send.at[i], recv_sem=disp_recv.at[i], device_id={"dp": d}, device_id_type=MESH)

    for i in range(N - 1):
        dispatch(i).start()
    q_own.wait()
    q_copy = pltpu.make_async_remote_copy(
        src_ref=q_all.at[0], dst_ref=q_all.at[1], send_sem=pair_send.at[0], recv_sem=pair_recv.at[0],
        device_id=sibling, device_id_type=MESH)
    q_copy.start()

    eye = jnp.where(iota((128, 128), 0) == iota((128, 128), 1), 1.0, 0.0).astype(BF16)
    for k in range(4):
        loads[2 * k].wait()
        loads[2 * k + 1].wait()

        def turn(n, carry, k=k):
            j = k * 4 + n
            for jj in (j, j + 16):
                flat = dot_t(eye, raw[jj, 0:KV, :])
                for i in range(4):
                    wide[pl.ds(i * POS + jj, 128, SLOT), :] = flat[:, i * 128 : (i + 1) * 128]
            rest = jnp.concatenate([raw[j, KV:, :], raw[j + 16, KV:, :]], axis=0)
            wide[pl.ds(4 * POS + j, 128, SLOT), :] = dot_t(eye, rest)
            return carry

        lax.fori_loop(0, 4, turn, 0)

    def exchange(i):
        d = peer(i, 1)
        return pltpu.make_async_remote_copy(
            src_ref=packed.at[d], dst_ref=resident.at[pl.ds(me * 2, 2)],
            send_sem=pool_send.at[i], recv_sem=pool_recv.at[i], device_id={"dp": d}, device_id_type=MESH)

    for i in range(N - 1):
        d = peer(i, 1)
        for h in range(2):
            packed[d, h] = wide[pl.ds(pl.multiple_of((d * 2 + h) * SLOT, SLOT), SLOT), :].astype(BF16)
        exchange(i).start()
    for h in range(2):
        resident[me * 2 + h] = wide[pl.ds(pl.multiple_of((me * 2 + h) * SLOT, SLOT), SLOT), :].astype(BF16)
    own = pl.ds(pl.multiple_of(me * ROW, ROW), ROW)
    in_rows[own, :] = out_rows[own, :]

    rr, cc = iota((N, N * ROW), 0), iota((N, N * ROW), 1)
    fits = (cc % ROW // 4 == rr // SESS) & (cc % 2 == rr % SESS // 8)
    shares = [jnp.where(before == j, weight, 0.0) for j in range(2)]
    for level in range(2):
        tops = [s.astype(BF16) for s in shares]
        picked = jnp.where(cc % 4 // 2 == 0, dot_t(spread(tops[0]), name), dot_t(spread(tops[1]), name))
        shares_of[level] = jnp.where(fits, picked, 0.0).astype(BF16)
        shares = [s - t_.astype(F32) for s, t_ in zip(shares, tops)]

    for i in range(N - 1):
        dispatch(i).wait()
    pair = pltpu.make_async_remote_copy(
        src_ref=in_rows, dst_ref=in_other, send_sem=pair_send.at[1], recv_sem=pair_recv.at[1],
        device_id=sibling, device_id_type=MESH)
    pair.start()
    r, c = iota((256, 256), 0), iota((256, 256), 1)
    order = r // 64 * 4 + r % 64 // 4 * 16 + r % 4
    gather = jnp.where(c == order, 1.0, 0.0).astype(BF16)
    scatter = jnp.where(r == c // 64 * 4 + c % 64 // 4 * 16 + c % 4, 1.0, 0.0).astype(BF16)
    for c_ in weights:
        c_.wait()
    gate_sum, up_sum = jnp.zeros((256, 512), F32), jnp.zeros((256, 512), F32)
    for side in range(2):
        if side == 1:
            pair.wait()
        rows_ref = (in_rows, in_other)[side]
        half = core if side == 0 else 1 - core
        lined = [dot(gather, rows_ref[k * 256 : (k + 1) * 256, :]).astype(BF16) for k in range(4)]
        for q, width in enumerate(WIDTHS):
            part = jnp.concatenate([lined[k][q * 64 : (q + 1) * 64, :width] for k in range(4)], axis=0)
            rows = pl.ds(pl.multiple_of(half * SLICE + q * CHUNK, 256), width)
            gate_sum += dot(part, wg[rows, :])
            up_sum += dot(part, wu[rows, :])
    hidden = (gate_sum / (1.0 + jnp.exp(-gate_sum)) * up_sum).astype(BF16)
    for q, width in enumerate(WIDTHS):
        columns = pl.ds(pl.multiple_of((1 - core) * SLICE + q * CHUNK, 256), width)
        share_out[:, q * CHUNK : q * CHUNK + width] = dot(hidden, wd[:, columns]).astype(BF16)
    share = pltpu.make_async_remote_copy(
        src_ref=share_out, dst_ref=share_in, send_sem=pair_send.at[2], recv_sem=pair_recv.at[2],
        device_id=sibling, device_id_type=MESH)
    share.start()
    mine = []
    for q, width in enumerate(WIDTHS):
        columns = pl.ds(pl.multiple_of(core * SLICE + q * CHUNK, 256), width)
        mine.append(dot(hidden, wd[:, columns]).astype(BF16))
    share.wait()
    full = []
    for q, width in enumerate(WIDTHS):
        total = (mine[q].astype(F32) + share_in[:, q * CHUNK : q * CHUNK + width].astype(F32)).astype(BF16)
        if width < CHUNK:
            total = jnp.concatenate([total, jnp.zeros((256, CHUNK - width), BF16)], axis=1)
        full.append(total)
    for k in range(4):
        stacked = jnp.concatenate([full[q][k * 64 : (k + 1) * 64] for q in range(4)], axis=0)
        back_rows[k * 256 : (k + 1) * 256, :] = dot(scatter, stacked).astype(BF16)

    def send_back(i):
        d = peer(i, 1)
        return pltpu.make_async_remote_copy(
            src_ref=back_rows.at[pl.ds(pl.multiple_of(d * ROW, ROW), ROW)],
            dst_ref=ret_rows.at[pl.ds(pl.multiple_of(me * ROW, ROW), ROW)],
            send_sem=back_send.at[i], recv_sem=back_recv.at[i], device_id={"dp": d}, device_id_type=MESH)

    for i in range(N - 1):
        exchange(i).wait_send()
    for i in range(N - 1):
        send_back(i).start()
    ret_rows[own, :] = back_rows[own, :]

    q_copy.wait()
    for i in range(N - 1):
        exchange(i).wait_recv()

    col = iota((2 * HEADS, 256), 1)
    position = col % 128 // 16 * 64 + core * POS + col // 128 * 16 + col % 16

    def parts(t):
        a = pltpu.make_async_remote_copy(
            src_ref=part_out.at[t], dst_ref=part_in.at[t], send_sem=part_send.at[t], recv_sem=part_recv.at[t],
            device_id=sibling, device_id_type=MESH)
        b = pltpu.make_async_remote_copy(
            src_ref=lse_out.at[t], dst_ref=lse_in.at[t], send_sem=lse_send.at[t], recv_sem=lse_recv.at[t],
            device_id=sibling, device_id_type=MESH)
        return a, b

    def attend(t, carry):
        low, high, rest = [], [], []
        for b in range(8):
            block = resident[table[t, b]]
            low.append(jnp.concatenate([block[i * POS : i * POS + 16] for i in range(4)], axis=1))
            high.append(jnp.concatenate([block[i * POS + 16 : i * POS + 32] for i in range(4)], axis=1))
            rest.append(block[4 * POS :])
        keys = jnp.concatenate(low + high, axis=0)
        rest = jnp.concatenate(rest, axis=0)
        q = jnp.concatenate([q_all[0, t], q_all[1, t]], axis=0)
        q_rest, blank = q[:, KV:], jnp.zeros((2 * HEADS, TAIL), BF16)
        scores = dot_t(q[:, :KV], keys) + jnp.concatenate(
            [dot_t(jnp.concatenate([q_rest, blank], axis=1), rest),
             dot_t(jnp.concatenate([blank, q_rest], axis=1), rest)], axis=1)
        inside = position < lengths[t // 8, t % 8]
        scores = jnp.where(inside, scores * SCALE, NEG)
        peak = jnp.max(scores, axis=1, keepdims=True)
        weights_ = jnp.where(inside, jnp.exp(scores - peak), 0.0)
        total = jnp.maximum(jnp.sum(weights_, axis=1, keepdims=True), 1e-30)
        value = dot(weights_.astype(BF16), keys) / total
        lse = jnp.broadcast_to(peak + jnp.log(total), (2 * HEADS, 128))
        part_own[t] = value[:HEADS]
        lse_own[t] = lse[:HEADS]
        part_out[t] = value[HEADS:].astype(BF16)
        lse_out[t] = lse[HEADS:]
        for copy in parts(t):
            copy.start()
        return carry

    lax.fori_loop(0, SESS, attend, 0, unroll=2)

    def merge(t, carry):
        for copy in parts(t):
            copy.wait()
        share_ = 1.0 / (1.0 + jnp.exp(lse_in[t] - lse_own[t]))
        share_ = jnp.concatenate([share_] * 4, axis=1)
        context[t] = (part_own[t] * share_ + part_in[t].astype(F32) * (1.0 - share_)).astype(BF16)
        return carry

    lax.fori_loop(0, SESS, merge, 0, unroll=2)

    for i in range(N - 1):
        send_back(i).wait()
    total = jnp.zeros((N, CHUNK), F32)
    for level in range(2):
        total += dot(shares_of[level], ret_rows[...])
    for q, width in enumerate(WIDTHS):
        moe[:, q * CHUNK : q * CHUNK + width] = total[q * SESS : (q + 1) * SESS, :width].astype(BF16)


def finish(context_in, moe_in, context, moe):
    context[...] = context_in[...]
    moe[...] = moe_in[...]


def on_device(pool, table, lengths, queries, hidden, ids, gates, w_gate, w_up, w_down):
    vmem = pl.BlockSpec(memory_space=pltpu.VMEM)
    smem = pl.BlockSpec(memory_space=pltpu.SMEM)
    anywhere = pl.BlockSpec(memory_space=pl.ANY)
    dma = pltpu.SemaphoreType.DMA
    context, moe = pl.pallas_call(
        kernel,
        out_shape=(
            jax.ShapeDtypeStruct((SESS, HEADS, KV), BF16),
            jax.ShapeDtypeStruct((SESS, SLICE), BF16),
        ),
        in_specs=[smem, smem, anywhere, anywhere, vmem, vmem, vmem, anywhere, anywhere, anywhere],
        out_specs=(vmem, vmem),
        scratch_shapes=[
            pltpu.VMEM((POS, KV + TAIL, 128), BF16),
            pltpu.VMEM((128 * SLOT, 128), F32),
            pltpu.VMEM((N, 2, SLOT, 128), BF16),
            pltpu.VMEM((128, SLOT, 128), BF16),
            pltpu.VMEM((2, SESS, HEADS, KV + TAIL), BF16),
            pltpu.VMEM((2 * SLICE, 512), BF16),
            pltpu.VMEM((2 * SLICE, 512), BF16),
            pltpu.VMEM((512, 2 * SLICE), BF16),
            pltpu.VMEM((N * ROW, CHUNK), BF16),
            pltpu.VMEM((N * ROW, CHUNK), BF16),
            pltpu.VMEM((N * ROW, CHUNK), BF16),
            pltpu.VMEM((256, SLICE), BF16),
            pltpu.VMEM((256, SLICE), BF16),
            pltpu.VMEM((N * ROW, CHUNK), BF16),
            pltpu.VMEM((N * ROW, CHUNK), BF16),
            pltpu.VMEM((SESS, HEADS, KV), F32),
            pltpu.VMEM((SESS, HEADS, 128), F32),
            pltpu.VMEM((SESS, HEADS, KV), BF16),
            pltpu.VMEM((SESS, HEADS, 128), F32),
            pltpu.VMEM((SESS, HEADS, KV), BF16),
            pltpu.VMEM((SESS, HEADS, 128), F32),
            pltpu.VMEM((2, N, N * ROW), BF16),
            dma((8,)), dma((3,)), dma((1,)),
            dma((N,)), dma((N,)), dma((N,)), dma((N,)), dma((N,)), dma((N,)),
            dma((3,)), dma((3,)),
            dma((SESS,)), dma((SESS,)), dma((SESS,)), dma((SESS,)),
        ],
        compiler_params=pltpu.CompilerParams(
            collective_id=0, has_side_effects=True, vmem_limit_bytes=60 * 2**20
        ),
    )(
        table.reshape(SESS, 8), lengths, pool.transpose(1, 2, 0),
        queries.reshape(SESS, HEADS, KV + TAIL), hidden.reshape(SESS, SLICE),
        ids.reshape(SESS, 8), gates.reshape(SESS, 8), w_gate[0], w_up[0], w_down[0],
    )
    context, moe = pl.pallas_call(
        finish,
        out_shape=(
            jax.ShapeDtypeStruct((SESS, HEADS, KV), BF16),
            jax.ShapeDtypeStruct((SESS, SLICE), BF16),
        ),
        grid=(4,),
        in_specs=[pl.BlockSpec((4, HEADS, KV), lambda i: (i, 0, 0)), pl.BlockSpec((SESS, SLICE), lambda i: (0, 0))],
        out_specs=(pl.BlockSpec((4, HEADS, KV), lambda i: (i, 0, 0)), pl.BlockSpec((SESS, SLICE), lambda i: (0, 0))),
    )(context, moe)
    return context.reshape(2, 8, HEADS, KV), moe.reshape(2, 8, SLICE)


def solution(mesh):
    placed = (
        P("dp", "inner", None),
        P(None, "dp", None),
        P(None, "dp"),
        P(None, "dp", "inner", None),
        P(None, "dp", "inner"),
        P(None, "dp", None),
        P(None, "dp", None),
        P("dp", None, "inner"),
        P("dp", None, "inner"),
        P("dp", "inner", None),
    )
    return jax.shard_map(
        on_device,
        mesh=mesh,
        in_specs=placed,
        out_specs=(P(None, "dp", "inner", None), P(None, "dp", "inner")),
        check_vma=False,
    )
```

```python
import functools

import jax
import jax.numpy as jnp
from jax import lax
from jax.experimental import pallas as pl
from jax.experimental.pallas import tpu as pltpu
from jax.sharding import PartitionSpec as P

MESH = pl.DeviceIdType.MESH
BF16, F32 = jnp.bfloat16, jnp.float32
SCALE = 192 ** (-0.5)
N = 64
POS = 32
KV, TAIL = 512, 64
SLOT = 144
SESS = 16
HEADS = 64
ROW = 16
CHUNK = 512
SLICE = 1792
NEG = -1e30
WIDTHS = (512, 512, 512, 256)
DIST = (0, 1, 2, 1)


def dot(a, b):
    return jnp.dot(a, b, preferred_element_type=F32)


def dot_t(a, b):
    return lax.dot_general(a, b, (((1,), (1,)), ((), ())), preferred_element_type=F32)


def target_orders():
    every = [(i % 4, i // 4 % 4, i // 16) for i in range(1, N)]
    kind = lambda o: tuple(sorted((DIST[a] for a in o), reverse=True))
    flip = lambda o: tuple(-a % 4 for a in o)
    turn = lambda o: (o[1], o[2], o[0])
    order = []
    for k in sorted({kind(o) for o in every}, key=lambda k: (-sum(k), k)):
        seen = []
        for o in every:
            if kind(o) != k or o in seen:
                continue
            for _ in range(3):
                for q in (o, flip(o)):
                    if q not in seen:
                        seen.append(q)
                o = turn(o)
        order += seen
    return order, [turn(o) for o in order]


ORDERS = target_orders()


def mixed(order):
    return [o for pair in zip(order, order[::-1]) for o in pair][: len(order)]


POOL_ORDERS = [mixed(order) for order in ORDERS]
BACK_ORDERS = [order[::-1] for order in ORDERS[::-1]]


def iota(shape, dim):
    return lax.broadcasted_iota(jnp.int32, shape, dim)


def kernel(
    table_in, lengths_in, pool, queries, tokens_in, ids_in, gates_in, w_gate, w_up, w_down,
    context, moe,
    table, lengths, tokens, ids, gates, merged, raw, wide, packed, resident, q_all, wg, wu, wd, out_rows, in_rows, in_other,
    share_out, share_in, back_rows, ret_rows, part_own, lse_own, part_out, lse_out, part_in, lse_in, shares_of,
    raw_sem, w_sem, q_sem, pool_send, pool_recv, disp_send, disp_recv, back_send, back_recv,
    pair_send, pair_recv, part_send, part_recv, lse_send, lse_recv, near_sem, far_sem, out_sem, small_sem,
):
    me = lax.axis_index("dp")
    core = lax.axis_index("inner")
    z, y, x = me // 16, me // 4 % 4, me % 4

    def shifted(o, sign):
        return (z + sign * o[2]) % 4 * 16 + (y + sign * o[1]) % 4 * 4 + (x + sign * o[0]) % 4

    def peer(i, orders=ORDERS):
        a, b = shifted(orders[0][i], 1), shifted(orders[1][i], 1)
        return a + core * (b - a)


    sibling = {"inner": 1 - core}

    barrier = pltpu.get_barrier_semaphore()

    line = []
    for k in range(1, 4):
        line += [shifted((k, 0, 0), 1), shifted((0, k, 0), 1), shifted((0, 0, k), 1)]

    def greet(semaphore):
        for d in line:
            pl.semaphore_signal(semaphore, inc=1, device_id={"dp": d}, device_id_type=MESH)

    pl.semaphore_signal(barrier, inc=1, device_id=sibling, device_id_type=MESH)
    greet(barrier)

    small = [
        pltpu.make_async_copy(a, b, small_sem.at[n])
        for n, (a, b) in enumerate(
            ((ids_in, ids), (tokens_in, tokens), (gates_in, gates), (table_in, table), (lengths_in, lengths)))
    ]
    for c in small:
        c.start()
    loads = []
    for k in range(4):
        for half in range(2):
            rows = pl.ds(half * 16 + k * 4, 4)
            loads.append(pltpu.make_async_copy(pool.at[rows], raw.at[rows], raw_sem.at[k * 2 + half]))
    for c in loads:
        c.start()
    q_own = pltpu.make_async_copy(queries, q_all.at[0], q_sem.at[0])
    q_own.start()
    weights = [
        pltpu.make_async_copy(a, b, w_sem.at[i]) for i, (a, b) in enumerate(((w_gate, wg), (w_up, wu), (w_down, wd)))
    ]
    for c in weights:
        c.start()

    for c in small:
        c.wait()

    experts = iota((SESS, N), 1)
    member, weight = jnp.zeros((SESS, N), F32), jnp.zeros((SESS, N), F32)
    for k in range(8):
        same = ids[:, k : k + 1] == experts
        member += jnp.where(same, 1.0, 0.0)
        weight += jnp.where(same, gates[:, k : k + 1], 0.0)
    r, c = iota((SESS, SESS), 0), iota((SESS, SESS), 1)
    before = dot(jnp.where((c < r) & (c // 8 == r // 8), 1.0, 0.0).astype(BF16), member.astype(BF16))
    tokens4 = jnp.concatenate(
        [tokens[:, 0:512], tokens[:, 512:1024], tokens[:, 1024:1536],
         jnp.concatenate([tokens[:, 1536:1792], jnp.zeros((SESS, 256), BF16)], axis=1)], axis=0)
    picks = [jnp.where(before == j, member, 0.0) for j in range(2)]
    name = jnp.where(iota((N * ROW, N), 0) // ROW == iota((N * ROW, N), 1), 1.0, 0.0).astype(BF16)

    def spread(m):
        return jnp.concatenate([m] * 4, axis=0).astype(BF16)

    rr, cc = iota((N * ROW, N), 0), iota((N * ROW, N), 1)
    fits = (rr % ROW // 4 == cc // SESS) & (rr % 2 == cc % SESS // 8)
    chosen = jnp.where(rr % 4 // 2 == 0, dot_t(name, spread(picks[0])), dot_t(name, spread(picks[1])))
    placing = jnp.where(fits, chosen, 0.0).astype(BF16)
    out_rows[...] = dot(placing, tokens4).astype(BF16)

    eye = jnp.where(iota((128, 128), 0) == iota((128, 128), 1), 1.0, 0.0).astype(BF16)

    def regroup(k):
        loads[2 * k].wait()
        loads[2 * k + 1].wait()

        def turn(n, carry):
            j = k * 4 + n
            for jj in (j, j + 16):
                flat = dot_t(eye, raw[jj, 0:KV, :])
                for i in range(4):
                    wide[pl.ds(i * POS + jj, 128, SLOT), :] = flat[:, i * 128 : (i + 1) * 128]
            rest = jnp.concatenate([raw[j, KV:, :], raw[j + 16, KV:, :]], axis=0)
            wide[pl.ds(4 * POS + j, 128, SLOT), :] = dot_t(eye, rest)
            return carry

        lax.fori_loop(0, 4, turn, 0)

    def dispatch(i):
        d = peer(i)
        return pltpu.make_async_remote_copy(
            src_ref=out_rows.at[pl.ds(pl.multiple_of(d * ROW, ROW), ROW)],
            dst_ref=in_rows.at[pl.ds(pl.multiple_of(me * ROW, ROW), ROW)],
            send_sem=disp_send.at[i], recv_sem=disp_recv.at[i], device_id={"dp": d}, device_id_type=MESH)

    def send_rows(moves):
        for i in range(N - 1):
            if sum(a > 0 for a in ORDERS[0][i]) == moves:
                dispatch(i).start()

    pl.semaphore_wait(barrier, 10)
    greet(near_sem)
    send_rows(1)
    q_own.wait()
    q_copy = pltpu.make_async_remote_copy(
        src_ref=q_all.at[0], dst_ref=q_all.at[1], send_sem=pair_send.at[0], recv_sem=pair_recv.at[0],
        device_id=sibling, device_id_type=MESH)
    q_copy.start()

    regroup(0)
    pl.semaphore_wait(near_sem, 9)
    greet(far_sem)
    send_rows(2)
    regroup(1)
    pl.semaphore_wait(far_sem, 9)
    send_rows(3)
    regroup(2)
    regroup(3)

    def exchange(i):
        d = peer(i, POOL_ORDERS)
        return pltpu.make_async_remote_copy(
            src_ref=packed.at[d], dst_ref=resident.at[pl.ds(me * 2, 2)],
            send_sem=pool_send.at[i], recv_sem=pool_recv.at[i], device_id={"dp": d}, device_id_type=MESH)

    for i in range(N - 1):
        d = peer(i, POOL_ORDERS)
        for h in range(2):
            packed[d, h] = wide[pl.ds(pl.multiple_of((d * 2 + h) * SLOT, SLOT), SLOT), :].astype(BF16)
        exchange(i).start()
    for h in range(2):
        resident[me * 2 + h] = wide[pl.ds(pl.multiple_of((me * 2 + h) * SLOT, SLOT), SLOT), :].astype(BF16)
    own = pl.ds(pl.multiple_of(me * ROW, ROW), ROW)
    in_rows[own, :] = out_rows[own, :]

    rr, cc = iota((N, N * ROW), 0), iota((N, N * ROW), 1)
    fits = (cc % ROW // 4 == rr // SESS) & (cc % 2 == rr % SESS // 8)
    shares = [jnp.where(before == j, weight, 0.0) for j in range(2)]
    for level in range(2):
        tops = [s.astype(BF16) for s in shares]
        picked = jnp.where(cc % 4 // 2 == 0, dot_t(spread(tops[0]), name), dot_t(spread(tops[1]), name))
        shares_of[level * N : (level + 1) * N, :] = jnp.where(fits, picked, 0.0).astype(BF16)
        shares = [s - t_.astype(F32) for s, t_ in zip(shares, tops)]

    for i in range(N - 1):
        dispatch(i).wait()
    pair = pltpu.make_async_remote_copy(
        src_ref=in_rows, dst_ref=in_other, send_sem=pair_send.at[1], recv_sem=pair_recv.at[1],
        device_id=sibling, device_id_type=MESH)
    pair.start()
    r, c = iota((256, 256), 0), iota((256, 256), 1)
    order = r // 64 * 4 + r % 64 // 4 * 16 + r % 4
    gather = jnp.where(c == order, 1.0, 0.0).astype(BF16)
    scatter = jnp.where(r == c // 64 * 4 + c % 64 // 4 * 16 + c % 4, 1.0, 0.0).astype(BF16)
    for c_ in weights:
        c_.wait()
    gate_sum, up_sum = jnp.zeros((256, 512), F32), jnp.zeros((256, 512), F32)
    for side in range(2):
        if side == 1:
            pair.wait()
        rows_ref = (in_rows, in_other)[side]
        half = core if side == 0 else 1 - core
        lined = [dot(gather, rows_ref[k * 256 : (k + 1) * 256, :]).astype(BF16) for k in range(4)]
        for q, width in enumerate(WIDTHS):
            part = jnp.concatenate([lined[k][q * 64 : (q + 1) * 64, :width] for k in range(4)], axis=0)
            rows = pl.ds(pl.multiple_of(half * SLICE + q * CHUNK, 256), width)
            gate_sum += dot(part, wg[rows, :])
            up_sum += dot(part, wu[rows, :])
    hidden = (gate_sum / (1.0 + jnp.exp(-gate_sum)) * up_sum).astype(BF16)
    for q, width in enumerate(WIDTHS):
        columns = pl.ds(pl.multiple_of((1 - core) * SLICE + q * CHUNK, 256), width)
        share_out[:, q * CHUNK : q * CHUNK + width] = dot(hidden, wd[:, columns]).astype(BF16)
    share = pltpu.make_async_remote_copy(
        src_ref=share_out, dst_ref=share_in, send_sem=pair_send.at[2], recv_sem=pair_recv.at[2],
        device_id=sibling, device_id_type=MESH)
    share.start()
    mine = []
    for q, width in enumerate(WIDTHS):
        columns = pl.ds(pl.multiple_of(core * SLICE + q * CHUNK, 256), width)
        mine.append(dot(hidden, wd[:, columns]).astype(BF16))
    share.wait()
    full = []
    for q, width in enumerate(WIDTHS):
        total = (mine[q].astype(F32) + share_in[:, q * CHUNK : q * CHUNK + width].astype(F32)).astype(BF16)
        if width < CHUNK:
            total = jnp.concatenate([total, jnp.zeros((256, CHUNK - width), BF16)], axis=1)
        full.append(total)
    for k in range(4):
        stacked = jnp.concatenate([full[q][k * 64 : (k + 1) * 64] for q in range(4)], axis=0)
        back_rows[k * 256 : (k + 1) * 256, :] = dot(scatter, stacked).astype(BF16)

    def send_back(i):
        d = peer(i, BACK_ORDERS)
        return pltpu.make_async_remote_copy(
            src_ref=back_rows.at[pl.ds(pl.multiple_of(d * ROW, ROW), ROW)],
            dst_ref=ret_rows.at[pl.ds(pl.multiple_of(me * ROW, ROW), ROW)],
            send_sem=back_send.at[i], recv_sem=back_recv.at[i], device_id={"dp": d}, device_id_type=MESH)

    for i in range(N - 1):
        exchange(i).wait_send()
    for i in range(N - 1):
        send_back(i).start()
    ret_rows[own, :] = back_rows[own, :]

    q_copy.wait()
    for i in range(N - 1):
        exchange(i).wait_recv()

    col = iota((2 * HEADS, 256), 1)
    position = col % 128 // 16 * 64 + core * POS + col // 128 * 16 + col % 16

    def parts(t):
        a = pltpu.make_async_remote_copy(
            src_ref=part_out.at[t], dst_ref=part_in.at[t], send_sem=part_send.at[t], recv_sem=part_recv.at[t],
            device_id=sibling, device_id_type=MESH)
        b = pltpu.make_async_remote_copy(
            src_ref=lse_out.at[t], dst_ref=lse_in.at[t], send_sem=lse_send.at[t], recv_sem=lse_recv.at[t],
            device_id=sibling, device_id_type=MESH)
        return a, b

    def attend(t, carry):
        low, high, rest = [], [], []
        for b in range(8):
            block = resident[table[t, b]]
            low.append(jnp.concatenate([block[i * POS : i * POS + 16] for i in range(4)], axis=1))
            high.append(jnp.concatenate([block[i * POS + 16 : i * POS + 32] for i in range(4)], axis=1))
            rest.append(block[4 * POS :])
        keys = jnp.concatenate(low + high, axis=0)
        rest = jnp.concatenate(rest, axis=0)
        q = jnp.concatenate([q_all[0, t], q_all[1, t]], axis=0)
        q_rest, blank = q[:, KV:], jnp.zeros((2 * HEADS, TAIL), BF16)
        scores = dot_t(q[:, :KV], keys) + jnp.concatenate(
            [dot_t(jnp.concatenate([q_rest, blank], axis=1), rest),
             dot_t(jnp.concatenate([blank, q_rest], axis=1), rest)], axis=1)
        inside = position < lengths[t // 8, t % 8]
        scores = jnp.where(inside, scores * SCALE, NEG)
        peak = jnp.max(scores, axis=1, keepdims=True)
        weights_ = jnp.where(inside, jnp.exp(scores - peak), 0.0)
        total = jnp.maximum(jnp.sum(weights_, axis=1, keepdims=True), 1e-30)
        value = dot(weights_.astype(BF16), keys) / total
        lse = jnp.broadcast_to(peak + jnp.log(total), (2 * HEADS, 128))
        part_own[t] = value[:HEADS]
        lse_own[t] = lse[:HEADS]
        part_out[t] = value[HEADS:].astype(BF16)
        lse_out[t] = lse[HEADS:]
        for copy in parts(t):
            copy.start()
        return carry

    lax.fori_loop(0, SESS, attend, 0, unroll=2)

    def merge(t, carry):
        for copy in parts(t):
            copy.wait()
        share_ = 1.0 / (1.0 + jnp.exp(lse_in[t] - lse_own[t]))
        share_ = jnp.concatenate([share_] * 4, axis=1)
        merged[t] = (part_own[t] * share_ + part_in[t].astype(F32) * (1.0 - share_)).astype(BF16)
        return carry

    lax.fori_loop(0, SESS, merge, 0, unroll=2)
    result = pltpu.make_async_copy(merged, context, out_sem.at[0])
    result.start()

    for i in range(N - 1):
        send_back(i).wait()
    both = dot(shares_of[...], ret_rows[...])
    total = both[:N] + both[N:]
    for q, width in enumerate(WIDTHS):
        moe[:, q * CHUNK : q * CHUNK + width] = total[q * SESS : (q + 1) * SESS, :width].astype(BF16)
    result.wait()


def finish(context_in, moe_in, context, moe, held, held_moe, in_sem, out_sem):
    steps = [(context_in.at[pl.ds(2 * k, 2)], held.at[pl.ds(2 * k, 2)], context.at[pl.ds(2 * k, 2)]) for k in range(8)]
    steps.append((moe_in, held_moe, moe))
    loads = [pltpu.make_async_copy(a, b, in_sem.at[k]) for k, (a, b, c) in enumerate(steps)]
    stores = [pltpu.make_async_copy(b, c, out_sem.at[k]) for k, (a, b, c) in enumerate(steps)]
    for c in loads:
        c.start()
    for load, store in zip(loads, stores):
        load.wait()
        store.start()
    for c in stores:
        c.wait()


def on_device(pool, table, lengths, queries, hidden, ids, gates, w_gate, w_up, w_down):
    vmem = pl.BlockSpec(memory_space=pltpu.VMEM)
    anywhere = pl.BlockSpec(memory_space=pl.ANY)
    dma = pltpu.SemaphoreType.DMA
    context, moe = pl.pallas_call(
        kernel,
        out_shape=(
            jax.ShapeDtypeStruct((SESS, HEADS, KV), BF16),
            jax.ShapeDtypeStruct((SESS, SLICE), BF16),
        ),
        in_specs=[anywhere] * 10,
        out_specs=(anywhere, vmem),
        scratch_shapes=[
            pltpu.SMEM((SESS, 8), jnp.int32),
            pltpu.SMEM((2, 8), jnp.int32),
            pltpu.VMEM((SESS, SLICE), BF16),
            pltpu.VMEM((SESS, 8), jnp.int32),
            pltpu.VMEM((SESS, 8), F32),
            pltpu.VMEM((SESS, HEADS, KV), BF16),
            pltpu.VMEM((POS, KV + TAIL, 128), BF16),
            pltpu.VMEM((128 * SLOT, 128), F32),
            pltpu.VMEM((N, 2, SLOT, 128), BF16),
            pltpu.VMEM((128, SLOT, 128), BF16),
            pltpu.VMEM((2, SESS, HEADS, KV + TAIL), BF16),
            pltpu.VMEM((2 * SLICE, 512), BF16),
            pltpu.VMEM((2 * SLICE, 512), BF16),
            pltpu.VMEM((512, 2 * SLICE), BF16),
            pltpu.VMEM((N * ROW, CHUNK), BF16),
            pltpu.VMEM((N * ROW, CHUNK), BF16),
            pltpu.VMEM((N * ROW, CHUNK), BF16),
            pltpu.VMEM((256, SLICE), BF16),
            pltpu.VMEM((256, SLICE), BF16),
            pltpu.VMEM((N * ROW, CHUNK), BF16),
            pltpu.VMEM((N * ROW, CHUNK), BF16),
            pltpu.VMEM((SESS, HEADS, KV), F32),
            pltpu.VMEM((SESS, HEADS, 128), F32),
            pltpu.VMEM((SESS, HEADS, KV), BF16),
            pltpu.VMEM((SESS, HEADS, 128), F32),
            pltpu.VMEM((SESS, HEADS, KV), BF16),
            pltpu.VMEM((SESS, HEADS, 128), F32),
            pltpu.VMEM((2 * N, N * ROW), BF16),
            dma((8,)), dma((3,)), dma((1,)),
            dma((N,)), dma((N,)), dma((N,)), dma((N,)), dma((N,)), dma((N,)),
            dma((3,)), dma((3,)),
            dma((SESS,)), dma((SESS,)), dma((SESS,)), dma((SESS,)),
            pltpu.SemaphoreType.REGULAR, pltpu.SemaphoreType.REGULAR, dma((1,)), dma((5,)),
        ],
        compiler_params=pltpu.CompilerParams(
            collective_id=0, has_side_effects=True, vmem_limit_bytes=60 * 2**20
        ),
    )(
        table.reshape(SESS, 8), lengths, pool.transpose(1, 2, 0),
        queries.reshape(SESS, HEADS, KV + TAIL), hidden.reshape(SESS, SLICE),
        ids.reshape(SESS, 8), gates.reshape(SESS, 8), w_gate[0], w_up[0], w_down[0],
    )
    context, moe = pl.pallas_call(
        finish,
        out_shape=(
            jax.ShapeDtypeStruct((SESS, HEADS, KV), BF16),
            jax.ShapeDtypeStruct((SESS, SLICE), BF16),
        ),
        in_specs=[anywhere, anywhere],
        out_specs=(anywhere, anywhere),
        scratch_shapes=[
            pltpu.VMEM((SESS, HEADS, KV), BF16), pltpu.VMEM((SESS, SLICE), BF16), dma((9,)), dma((9,)),
        ],
    )(context, moe)
    return context.reshape(2, 8, HEADS, KV), moe.reshape(2, 8, SLICE)


def solution(mesh):
    placed = (
        P("dp", "inner", None),
        P(None, "dp", None),
        P(None, "dp"),
        P(None, "dp", "inner", None),
        P(None, "dp", "inner"),
        P(None, "dp", None),
        P(None, "dp", None),
        P("dp", None, "inner"),
        P("dp", None, "inner"),
        P("dp", "inner", None),
    )
    return jax.shard_map(
        on_device,
        mesh=mesh,
        in_specs=placed,
        out_specs=(P(None, "dp", "inner", None), P(None, "dp", "inner")),
        check_vma=False,
    )
```

```python
import functools

import jax
import jax.numpy as jnp
from jax import lax
from jax.experimental import pallas as pl
from jax.experimental.pallas import tpu as pltpu
from jax.sharding import PartitionSpec as P

MESH = pl.DeviceIdType.MESH
BF16, F32 = jnp.bfloat16, jnp.float32
SCALE = 192 ** (-0.5)
N = 64
POS = 32
KV, TAIL = 512, 64
SLOT = 144
SESS = 16
HEADS = 64
ROW = 16
CHUNK = 512
SLICE = 1792
NEG = -1e30
WIDTHS = (512, 512, 512, 256)
DIST = (0, 1, 2, 1)


def dot(a, b):
    return jnp.dot(a, b, preferred_element_type=F32)


def dot_t(a, b):
    return lax.dot_general(a, b, (((1,), (1,)), ((), ())), preferred_element_type=F32)


def target_orders():
    every = [(i % 4, i // 4 % 4, i // 16) for i in range(1, N)]
    kind = lambda o: tuple(sorted((DIST[a] for a in o), reverse=True))
    flip = lambda o: tuple(-a % 4 for a in o)
    turn = lambda o: (o[1], o[2], o[0])
    order = []
    for k in sorted({kind(o) for o in every}, key=lambda k: (-sum(k), k)):
        seen = []
        for o in every:
            if kind(o) != k or o in seen:
                continue
            for _ in range(3):
                for q in (o, flip(o)):
                    if q not in seen:
                        seen.append(q)
                o = turn(o)
        order += seen
    return order, [turn(o) for o in order]


ORDERS = target_orders()


def mixed(order):
    return [o for pair in zip(order, order[::-1]) for o in pair][: len(order)]


POOL_ORDERS = [mixed(order) for order in ORDERS]
BACK_ORDERS = [ORDERS[1][::-1], [tuple(-a % 4 for a in o) for o in ORDERS[0][::-1]]]


def iota(shape, dim):
    return lax.broadcasted_iota(jnp.int32, shape, dim)


def kernel(
    table_in, lengths_in, pool, queries, tokens_in, ids_in, gates_in, w_gate, w_up, w_down,
    context, moe,
    table, lengths, tokens, ids, gates, merged, raw, wide, packed, resident, q_all, wg, wu, wd, out_rows, in_rows, in_other,
    share_out, share_in, back_rows, ret_rows, part_own, lse_own, part_out, lse_out, part_in, lse_in, shares_of,
    raw_sem, w_sem, q_sem, pool_send, pool_recv, disp_send, disp_recv, back_send, back_recv,
    pair_send, pair_recv, part_send, part_recv, lse_send, lse_recv, near_sem, far_sem, out_sem, small_sem,
):
    me = lax.axis_index("dp")
    core = lax.axis_index("inner")
    z, y, x = me // 16, me // 4 % 4, me % 4

    def shifted(o, sign):
        return (z + sign * o[2]) % 4 * 16 + (y + sign * o[1]) % 4 * 4 + (x + sign * o[0]) % 4

    def peer(i, orders=ORDERS):
        a, b = shifted(orders[0][i], 1), shifted(orders[1][i], 1)
        return a + core * (b - a)


    sibling = {"inner": 1 - core}

    barrier = pltpu.get_barrier_semaphore()

    line = []
    for k in range(1, 4):
        line += [shifted((k, 0, 0), 1), shifted((0, k, 0), 1), shifted((0, 0, k), 1)]

    def greet(semaphore):
        for d in line:
            pl.semaphore_signal(semaphore, inc=1, device_id={"dp": d}, device_id_type=MESH)

    pl.semaphore_signal(barrier, inc=1, device_id=sibling, device_id_type=MESH)
    greet(barrier)

    small = [
        pltpu.make_async_copy(a, b, small_sem.at[n])
        for n, (a, b) in enumerate(
            ((ids_in, ids), (tokens_in, tokens), (gates_in, gates), (table_in, table), (lengths_in, lengths)))
    ]
    for c in small:
        c.start()
    loads = []
    for k in range(4):
        for half in range(2):
            rows = pl.ds(half * 16 + k * 4, 4)
            loads.append(pltpu.make_async_copy(pool.at[rows], raw.at[rows], raw_sem.at[k * 2 + half]))
    for c in loads:
        c.start()
    q_own = pltpu.make_async_copy(queries, q_all.at[0], q_sem.at[0])
    q_own.start()
    weights = [
        pltpu.make_async_copy(a, b, w_sem.at[i]) for i, (a, b) in enumerate(((w_gate, wg), (w_up, wu), (w_down, wd)))
    ]
    for c in weights:
        c.start()

    for c in small:
        c.wait()

    experts = iota((SESS, N), 1)
    member, weight = jnp.zeros((SESS, N), F32), jnp.zeros((SESS, N), F32)
    for k in range(8):
        same = ids[:, k : k + 1] == experts
        member += jnp.where(same, 1.0, 0.0)
        weight += jnp.where(same, gates[:, k : k + 1], 0.0)
    r, c = iota((SESS, SESS), 0), iota((SESS, SESS), 1)
    before = dot(jnp.where((c < r) & (c // 8 == r // 8), 1.0, 0.0).astype(BF16), member.astype(BF16))
    tokens4 = jnp.concatenate(
        [tokens[:, 0:512], tokens[:, 512:1024], tokens[:, 1024:1536],
         jnp.concatenate([tokens[:, 1536:1792], jnp.zeros((SESS, 256), BF16)], axis=1)], axis=0)
    picks = [jnp.where(before == j, member, 0.0) for j in range(2)]
    name = jnp.where(iota((N * ROW, N), 0) // ROW == iota((N * ROW, N), 1), 1.0, 0.0).astype(BF16)

    def spread(m):
        return jnp.concatenate([m] * 4, axis=0).astype(BF16)

    rr, cc = iota((N * ROW, N), 0), iota((N * ROW, N), 1)
    fits = (rr % ROW // 4 == cc // SESS) & (rr % 2 == cc % SESS // 8)
    chosen = jnp.where(rr % 4 // 2 == 0, dot_t(name, spread(picks[0])), dot_t(name, spread(picks[1])))
    placing = jnp.where(fits, chosen, 0.0).astype(BF16)
    out_rows[...] = dot(placing, tokens4).astype(BF16)

    eye = jnp.where(iota((128, 128), 0) == iota((128, 128), 1), 1.0, 0.0).astype(BF16)

    def regroup(k):
        loads[2 * k].wait()
        loads[2 * k + 1].wait()

        def turn(n, carry):
            j = k * 4 + n
            for jj in (j, j + 16):
                flat = dot_t(eye, raw[jj, 0:KV, :])
                for i in range(4):
                    wide[pl.ds(i * POS + jj, 128, SLOT), :] = flat[:, i * 128 : (i + 1) * 128]
            rest = jnp.concatenate([raw[j, KV:, :], raw[j + 16, KV:, :]], axis=0)
            wide[pl.ds(4 * POS + j, 128, SLOT), :] = dot_t(eye, rest)
            return carry

        lax.fori_loop(0, 4, turn, 0)

    def dispatch(i):
        d = peer(i)
        return pltpu.make_async_remote_copy(
            src_ref=out_rows.at[pl.ds(pl.multiple_of(d * ROW, ROW), ROW)],
            dst_ref=in_rows.at[pl.ds(pl.multiple_of(me * ROW, ROW), ROW)],
            send_sem=disp_send.at[i], recv_sem=disp_recv.at[i], device_id={"dp": d}, device_id_type=MESH)

    def send_rows(moves):
        for i in range(N - 1):
            if sum(a > 0 for a in ORDERS[0][i]) == moves:
                dispatch(i).start()

    pl.semaphore_wait(barrier, 10)
    greet(near_sem)
    send_rows(1)
    q_own.wait()
    q_copy = pltpu.make_async_remote_copy(
        src_ref=q_all.at[0], dst_ref=q_all.at[1], send_sem=pair_send.at[0], recv_sem=pair_recv.at[0],
        device_id=sibling, device_id_type=MESH)
    q_copy.start()

    regroup(0)
    pl.semaphore_wait(near_sem, 9)
    greet(far_sem)
    send_rows(2)
    regroup(1)
    pl.semaphore_wait(far_sem, 9)
    send_rows(3)
    regroup(2)
    regroup(3)

    def exchange(i):
        d = peer(i, POOL_ORDERS)
        return pltpu.make_async_remote_copy(
            src_ref=packed.at[d], dst_ref=resident.at[pl.ds(me * 2, 2)],
            send_sem=pool_send.at[i], recv_sem=pool_recv.at[i], device_id={"dp": d}, device_id_type=MESH)

    for i in range(N - 1):
        d = peer(i, POOL_ORDERS)
        for h in range(2):
            packed[d, h] = wide[pl.ds(pl.multiple_of((d * 2 + h) * SLOT, SLOT), SLOT), :].astype(BF16)
        exchange(i).start()
    for h in range(2):
        resident[me * 2 + h] = wide[pl.ds(pl.multiple_of((me * 2 + h) * SLOT, SLOT), SLOT), :].astype(BF16)
    own = pl.ds(pl.multiple_of(me * ROW, ROW), ROW)
    in_rows[own, :] = out_rows[own, :]

    rr, cc = iota((N, N * ROW), 0), iota((N, N * ROW), 1)
    fits = (cc % ROW // 4 == rr // SESS) & (cc % 2 == rr % SESS // 8)
    shares = [jnp.where(before == j, weight, 0.0) for j in range(2)]
    for level in range(2):
        tops = [s.astype(BF16) for s in shares]
        picked = jnp.where(cc % 4 // 2 == 0, dot_t(spread(tops[0]), name), dot_t(spread(tops[1]), name))
        shares_of[level * N : (level + 1) * N, :] = jnp.where(fits, picked, 0.0).astype(BF16)
        shares = [s - t_.astype(F32) for s, t_ in zip(shares, tops)]

    for i in range(N - 1):
        dispatch(i).wait()
    pair = pltpu.make_async_remote_copy(
        src_ref=in_rows, dst_ref=in_other, send_sem=pair_send.at[1], recv_sem=pair_recv.at[1],
        device_id=sibling, device_id_type=MESH)
    pair.start()
    r, c = iota((256, 256), 0), iota((256, 256), 1)
    order = r // 64 * 4 + r % 64 // 4 * 16 + r % 4
    gather = jnp.where(c == order, 1.0, 0.0).astype(BF16)
    scatter = jnp.where(r == c // 64 * 4 + c % 64 // 4 * 16 + c % 4, 1.0, 0.0).astype(BF16)
    for c_ in weights:
        c_.wait()
    gate_sum, up_sum = jnp.zeros((256, 512), F32), jnp.zeros((256, 512), F32)
    for side in range(2):
        if side == 1:
            pair.wait()
        rows_ref = (in_rows, in_other)[side]
        half = core if side == 0 else 1 - core
        lined = [dot(gather, rows_ref[k * 256 : (k + 1) * 256, :]).astype(BF16) for k in range(4)]
        for q, width in enumerate(WIDTHS):
            part = jnp.concatenate([lined[k][q * 64 : (q + 1) * 64, :width] for k in range(4)], axis=0)
            rows = pl.ds(pl.multiple_of(half * SLICE + q * CHUNK, 256), width)
            gate_sum += dot(part, wg[rows, :])
            up_sum += dot(part, wu[rows, :])
    hidden = (gate_sum / (1.0 + jnp.exp(-gate_sum)) * up_sum).astype(BF16)
    for q, width in enumerate(WIDTHS):
        columns = pl.ds(pl.multiple_of((1 - core) * SLICE + q * CHUNK, 256), width)
        share_out[:, q * CHUNK : q * CHUNK + width] = dot(hidden, wd[:, columns]).astype(BF16)
    share = pltpu.make_async_remote_copy(
        src_ref=share_out, dst_ref=share_in, send_sem=pair_send.at[2], recv_sem=pair_recv.at[2],
        device_id=sibling, device_id_type=MESH)
    share.start()
    mine = []
    for q, width in enumerate(WIDTHS):
        columns = pl.ds(pl.multiple_of(core * SLICE + q * CHUNK, 256), width)
        mine.append(dot(hidden, wd[:, columns]).astype(BF16))
    share.wait()
    full = []
    for q, width in enumerate(WIDTHS):
        total = (mine[q].astype(F32) + share_in[:, q * CHUNK : q * CHUNK + width].astype(F32)).astype(BF16)
        if width < CHUNK:
            total = jnp.concatenate([total, jnp.zeros((256, CHUNK - width), BF16)], axis=1)
        full.append(total)
    for k in range(4):
        stacked = jnp.concatenate([full[q][k * 64 : (k + 1) * 64] for q in range(4)], axis=0)
        back_rows[k * 256 : (k + 1) * 256, :] = dot(scatter, stacked).astype(BF16)

    def send_back(i):
        d = peer(i, BACK_ORDERS)
        return pltpu.make_async_remote_copy(
            src_ref=back_rows.at[pl.ds(pl.multiple_of(d * ROW, ROW), ROW)],
            dst_ref=ret_rows.at[pl.ds(pl.multiple_of(me * ROW, ROW), ROW)],
            send_sem=back_send.at[i], recv_sem=back_recv.at[i], device_id={"dp": d}, device_id_type=MESH)

    for i in range(N - 1):
        exchange(i).wait_send()
    for i in range(N - 1):
        send_back(i).start()
    ret_rows[own, :] = back_rows[own, :]

    q_copy.wait()
    for i in range(N - 1):
        exchange(i).wait_recv()

    col = iota((2 * HEADS, 256), 1)
    position = col % 128 // 16 * 64 + core * POS + col // 128 * 16 + col % 16

    def parts(t):
        a = pltpu.make_async_remote_copy(
            src_ref=part_out.at[t], dst_ref=part_in.at[t], send_sem=part_send.at[t], recv_sem=part_recv.at[t],
            device_id=sibling, device_id_type=MESH)
        b = pltpu.make_async_remote_copy(
            src_ref=lse_out.at[t], dst_ref=lse_in.at[t], send_sem=lse_send.at[t], recv_sem=lse_recv.at[t],
            device_id=sibling, device_id_type=MESH)
        return a, b

    def attend(t, carry):
        low, high, rest = [], [], []
        for b in range(8):
            block = resident[table[t, b]]
            low.append(jnp.concatenate([block[i * POS : i * POS + 16] for i in range(4)], axis=1))
            high.append(jnp.concatenate([block[i * POS + 16 : i * POS + 32] for i in range(4)], axis=1))
            rest.append(block[4 * POS :])
        keys = jnp.concatenate(low + high, axis=0)
        rest = jnp.concatenate(rest, axis=0)
        q = jnp.concatenate([q_all[0, t], q_all[1, t]], axis=0)
        q_rest, blank = q[:, KV:], jnp.zeros((2 * HEADS, TAIL), BF16)
        scores = dot_t(q[:, :KV], keys) + jnp.concatenate(
            [dot_t(jnp.concatenate([q_rest, blank], axis=1), rest),
             dot_t(jnp.concatenate([blank, q_rest], axis=1), rest)], axis=1)
        inside = position < lengths[t // 8, t % 8]
        scores = jnp.where(inside, scores * SCALE, NEG)
        peak = jnp.max(scores, axis=1, keepdims=True)
        weights_ = jnp.where(inside, jnp.exp(scores - peak), 0.0)
        total = jnp.maximum(jnp.sum(weights_, axis=1, keepdims=True), 1e-30)
        value = dot(weights_.astype(BF16), keys) / total
        lse = jnp.broadcast_to(peak + jnp.log(total), (2 * HEADS, 128))
        part_own[t] = value[:HEADS]
        lse_own[t] = lse[:HEADS]
        part_out[t] = value[HEADS:].astype(BF16)
        lse_out[t] = lse[HEADS:]
        for copy in parts(t):
            copy.start()
        return carry

    lax.fori_loop(0, SESS, attend, 0, unroll=2)

    def merge(t, carry):
        for copy in parts(t):
            copy.wait()
        share_ = 1.0 / (1.0 + jnp.exp(lse_in[t] - lse_own[t]))
        share_ = jnp.concatenate([share_] * 4, axis=1)
        merged[t] = (part_own[t] * share_ + part_in[t].astype(F32) * (1.0 - share_)).astype(BF16)
        return carry

    lax.fori_loop(0, SESS, merge, 0, unroll=2)
    result = pltpu.make_async_copy(merged, context, out_sem.at[0])
    result.start()

    for i in range(N - 1):
        send_back(i).wait()
    both = dot(shares_of[...], ret_rows[...])
    total = both[:N] + both[N:]
    for q, width in enumerate(WIDTHS):
        moe[:, q * CHUNK : q * CHUNK + width] = total[q * SESS : (q + 1) * SESS, :width].astype(BF16)
    result.wait()


def finish(context_in, moe_in, context, moe, held, held_moe, in_sem, out_sem):
    steps = [(context_in.at[pl.ds(2 * k, 2)], held.at[pl.ds(2 * k, 2)], context.at[pl.ds(2 * k, 2)]) for k in range(8)]
    steps.append((moe_in, held_moe, moe))
    loads = [pltpu.make_async_copy(a, b, in_sem.at[k]) for k, (a, b, c) in enumerate(steps)]
    stores = [pltpu.make_async_copy(b, c, out_sem.at[k]) for k, (a, b, c) in enumerate(steps)]
    for c in loads:
        c.start()
    for load, store in zip(loads, stores):
        load.wait()
        store.start()
    for c in stores:
        c.wait()


def on_device(pool, table, lengths, queries, hidden, ids, gates, w_gate, w_up, w_down):
    vmem = pl.BlockSpec(memory_space=pltpu.VMEM)
    anywhere = pl.BlockSpec(memory_space=pl.ANY)
    dma = pltpu.SemaphoreType.DMA
    context, moe = pl.pallas_call(
        kernel,
        out_shape=(
            jax.ShapeDtypeStruct((SESS, HEADS, KV), BF16),
            jax.ShapeDtypeStruct((SESS, SLICE), BF16),
        ),
        in_specs=[anywhere] * 10,
        out_specs=(anywhere, vmem),
        scratch_shapes=[
            pltpu.SMEM((SESS, 8), jnp.int32),
            pltpu.SMEM((2, 8), jnp.int32),
            pltpu.VMEM((SESS, SLICE), BF16),
            pltpu.VMEM((SESS, 8), jnp.int32),
            pltpu.VMEM((SESS, 8), F32),
            pltpu.VMEM((SESS, HEADS, KV), BF16),
            pltpu.VMEM((POS, KV + TAIL, 128), BF16),
            pltpu.VMEM((128 * SLOT, 128), F32),
            pltpu.VMEM((N, 2, SLOT, 128), BF16),
            pltpu.VMEM((128, SLOT, 128), BF16),
            pltpu.VMEM((2, SESS, HEADS, KV + TAIL), BF16),
            pltpu.VMEM((2 * SLICE, 512), BF16),
            pltpu.VMEM((2 * SLICE, 512), BF16),
            pltpu.VMEM((512, 2 * SLICE), BF16),
            pltpu.VMEM((N * ROW, CHUNK), BF16),
            pltpu.VMEM((N * ROW, CHUNK), BF16),
            pltpu.VMEM((N * ROW, CHUNK), BF16),
            pltpu.VMEM((256, SLICE), BF16),
            pltpu.VMEM((256, SLICE), BF16),
            pltpu.VMEM((N * ROW, CHUNK), BF16),
            pltpu.VMEM((N * ROW, CHUNK), BF16),
            pltpu.VMEM((SESS, HEADS, KV), F32),
            pltpu.VMEM((SESS, HEADS, 128), F32),
            pltpu.VMEM((SESS, HEADS, KV), BF16),
            pltpu.VMEM((SESS, HEADS, 128), F32),
            pltpu.VMEM((SESS, HEADS, KV), BF16),
            pltpu.VMEM((SESS, HEADS, 128), F32),
            pltpu.VMEM((2 * N, N * ROW), BF16),
            dma((8,)), dma((3,)), dma((1,)),
            dma((N,)), dma((N,)), dma((N,)), dma((N,)), dma((N,)), dma((N,)),
            dma((3,)), dma((3,)),
            dma((SESS,)), dma((SESS,)), dma((SESS,)), dma((SESS,)),
            pltpu.SemaphoreType.REGULAR, pltpu.SemaphoreType.REGULAR, dma((1,)), dma((5,)),
        ],
        compiler_params=pltpu.CompilerParams(
            collective_id=0, has_side_effects=True, vmem_limit_bytes=60 * 2**20
        ),
    )(
        table.reshape(SESS, 8), lengths, pool.transpose(1, 2, 0),
        queries.reshape(SESS, HEADS, KV + TAIL), hidden.reshape(SESS, SLICE),
        ids.reshape(SESS, 8), gates.reshape(SESS, 8), w_gate[0], w_up[0], w_down[0],
    )
    context, moe = pl.pallas_call(
        finish,
        out_shape=(
            jax.ShapeDtypeStruct((SESS, HEADS, KV), BF16),
            jax.ShapeDtypeStruct((SESS, SLICE), BF16),
        ),
        in_specs=[anywhere, anywhere],
        out_specs=(anywhere, anywhere),
        scratch_shapes=[
            pltpu.VMEM((SESS, HEADS, KV), BF16), pltpu.VMEM((SESS, SLICE), BF16), dma((9,)), dma((9,)),
        ],
    )(context, moe)
    return context.reshape(2, 8, HEADS, KV), moe.reshape(2, 8, SLICE)


def solution(mesh):
    placed = (
        P("dp", "inner", None),
        P(None, "dp", None),
        P(None, "dp"),
        P(None, "dp", "inner", None),
        P(None, "dp", "inner"),
        P(None, "dp", None),
        P(None, "dp", None),
        P("dp", None, "inner"),
        P("dp", None, "inner"),
        P("dp", "inner", None),
    )
    return jax.shard_map(
        on_device,
        mesh=mesh,
        in_specs=placed,
        out_specs=(P(None, "dp", "inner", None), P(None, "dp", "inner")),
        check_vma=False,
    )
```
